32 devices in a mesh: grp: 4 (over y, x), line: 8 (over z, core).
Axes of the slice: x: 2, y: 2, z: 4, core: 2. Of those that a mesh axis runs over, the one named last changes fastest.
Arguments:
- raw_echo: bfloat16 [2, 4096, 65536], P(None, ('grp', 'line')), may hold values from -6 to 6
- valid_lines: int32 [32], replicated, may hold values from 1 to 128, as said below
- range_filter: float32 [2, 65536], replicated, may hold values from -5 to 5
- azimuth_filters: float32 [2, 16, 4096], replicated, may hold values from -5 to 5
- set_index: int32 [65536], replicated, may hold values from 0 to 15, never falling along the last dimension, each value on 1 to 8192 neighbouring positions
Outputs:
- focused: bfloat16 [2, 4096, 65536], P(None, ('grp', 'line'))
The draws below stay inside these ranges and needn't reach their ends.
Inputs may be any that keep to these rules, and one draw needn't show every extreme that they name: For every block b with b % (8) < 4, valid_lines[b] + valid_lines[b + 4] <= 160; in every draw one such pair holds exactly 128 and 32. `set_index`: never falls along the range.
All inputs are finite; a program needn't handle non-finite values.
Results may differ from the reference program's by a relative error of at most 0.014.
Values may be sent and summed in bfloat16 or wider, within the bound.
A program may use at most 320 MiB of HBM per device.

```python
import math
import jax
import jax.numpy as jnp
import numpy as np
from jax import lax

LINES = 4096
RANGE = 65536
RANGE_LO = 256
AZ_INNER = 64
SETS = 16
RANGE_HI = 256
BLOCKS = 32
LINES_DEV = 128
HALF = 4
AZ_OUTER = 64
COLS = 2048
CAP = 80


def draw_valid_lines(key, part):
    pair_total = BLOCKS // 2
    key_heavy, key_light, key_side = jax.random.split(key, 3)
    heavy_count = jax.random.randint(key_heavy, (pair_total,), CAP, LINES_DEV + 1, dtype=jnp.int32)
    heavy_count = heavy_count.at[0].set(LINES_DEV)
    light_count = jax.random.randint(key_light, (pair_total,), 1, 2 * CAP - heavy_count + 1, dtype=jnp.int32)
    light_count = light_count.at[0].set(2 * CAP - LINES_DEV)
    side_bits = jax.random.randint(key_side, (pair_total,), 0, 2, dtype=jnp.int32)
    pair_ids = jnp.arange(pair_total, dtype=jnp.int32)
    first_ids = pair_ids // HALF * (2 * HALF) + pair_ids % HALF
    second_ids = first_ids + HALF
    counts = jnp.zeros((BLOCKS,), jnp.int32)
    counts = counts.at[first_ids].set(jnp.where(side_bits == 1, heavy_count, light_count))
    counts = counts.at[second_ids].set(jnp.where(side_bits == 1, light_count, heavy_count))
    return counts


def level_of(key, extent, cuts, low, top_value):
    loudness = 1.0
    for position, parts in cuts:
        heights = jax.random.uniform(jax.random.fold_in(jax.random.fold_in(key, 6), position), (parts,), jnp.float32, low / len(cuts), top_value / len(cuts))
        loudness = loudness * jnp.repeat(jnp.exp(heights), extent[position] // parts).reshape((-1,) + (1,) * (len(extent) - 1 - position))
    return loudness


def split_up(amount, total, bound, lean):
    loads = [(1 << 20) // math.isqrt(standing ** lean) + 1 for standing in range(2, amount + 1)]
    rest, holding = total - bound - (amount - 1), [1] * (amount - 1)
    while rest > 0:
        movable = [i for i in range(amount - 1) if holding[i] < bound]
        whole, budget = sum([loads[i] for i in movable]), rest
        for i in movable:
            more = min(bound - holding[i], max(1, budget * loads[i] // whole), rest)
            holding[i] = holding[i] + more
            rest = rest - more
    return np.array([bound] + holding)


def uneven(key, number_of, total, reach, lean):
    if number_of == 2:
        one = jax.random.randint(key, (), max(1, total - reach), min(reach, total - 1) + 1)
        return jnp.stack([one, total - one])
    sizes = jnp.asarray(split_up(number_of, total, reach, lean), jnp.int32)
    pairs = (number_of - 1) // 2
    donor, taker = sizes[1:1 + 2 * pairs:2], sizes[2:2 + 2 * pairs:2]
    margin = jnp.minimum(donor - 1, reach - taker)
    passed = jax.random.randint(jax.random.fold_in(key, 1), (pairs,), 0, 1 << 20) % (margin + 1)
    sizes = sizes.at[1:1 + 2 * pairs:2].set(donor - passed).at[2:2 + 2 * pairs:2].set(taker + passed)
    return sizes[jax.random.permutation(jax.random.fold_in(key, 2), number_of)]


def gaussian(own_key, dims, width, limit, cuts=(), kind=jnp.bfloat16):
    values = jax.random.normal(own_key, dims, jnp.float32) * width
    if len(cuts) > 0:
        values = level_of(own_key, dims, cuts, -0.22, 0.18) * values
    return jnp.clip(values, min=-limit, max=limit).astype(kind)


def setup_inputs(seed: int = 0) -> dict:
    key_list = jax.random.split(jax.random.key(seed), 6)
    return {
        "raw_echo": gaussian(key_list[0], (2, LINES, RANGE), 1.0, 6.0, ((1, 32),)),
        "valid_lines": draw_valid_lines(jax.random.fold_in(key_list[5], 71), 0),
        "range_filter": gaussian(key_list[2], (2, RANGE), 0.7, 5.0, (), jnp.float32),
        "azimuth_filters": gaussian(key_list[3], (2, SETS, LINES), 0.7, 5.0, (), jnp.float32),
        "set_index": jnp.searchsorted(jnp.cumsum(uneven(key_list[4], SETS, RANGE, 2 * RANGE // SETS, 0)), jnp.arange(RANGE), side="right").astype(jnp.int32),
    }


def fourier_table(length, sign_value):
    indices = jnp.arange(length, dtype=jnp.int32)
    phases = indices[:, None] * indices[None, :] % length
    angles = phases.astype(jnp.float32) * (2.0 * math.pi / length)
    cosine = jnp.cos(angles)
    sine_part = sign_value * jnp.sin(angles)
    top_rows = jnp.stack([cosine, -sine_part], axis=1)
    low_rows = jnp.stack([sine_part, cosine], axis=1)
    return jnp.stack([top_rows, low_rows], axis=0).astype(jnp.bfloat16)

def twiddle(row_len, col_len, total_len, sign_value):
    phases = jnp.arange(row_len, dtype=jnp.int32)[:, None] * jnp.arange(col_len, dtype=jnp.int32)[None, :] % total_len
    angles = phases.astype(jnp.float32) * (2.0 * math.pi / total_len)
    factor = 1.0 / math.sqrt(total_len)
    return (jnp.cos(angles) * factor, sign_value * jnp.sin(angles) * factor)

def rotate(values, cosine, sine_part):
    return jnp.stack([cosine * values[0] - sine_part * values[1], sine_part * values[0] + cosine * values[1]], axis=0)

def product(spec, left, right):
    return jnp.einsum(spec, left.astype(jnp.float32), right.astype(jnp.float32), precision=lax.Precision.HIGHEST)

def compress_lines(block, live_rows, range_filter):
    line_total = block.shape[1]
    high_len = RANGE_HI
    low_len = RANGE_LO
    grid_data = block.reshape(2, line_total, high_len, low_len)
    section_one = product('dkcn,clnb->dlkb', fourier_table(high_len, -1.0), grid_data)
    cosine, sine_part = twiddle(high_len, low_len, RANGE, -1.0)
    rotated = rotate(section_one, cosine, sine_part).astype(jnp.bfloat16)
    spectrum = product('dkcn,clan->dlak', fourier_table(low_len, -1.0), rotated)
    filter_grid = range_filter.reshape(2, low_len, high_len).transpose(0, 2, 1)
    shaped = jnp.stack([spectrum[0] * filter_grid[0] - spectrum[1] * filter_grid[1], spectrum[0] * filter_grid[1] + spectrum[1] * filter_grid[0]], axis=0).astype(jnp.bfloat16)
    back_section = product('dnck,clak->dlan', fourier_table(low_len, 1.0), shaped)
    cosine, sine_part = twiddle(high_len, low_len, RANGE, 1.0)
    turned = rotate(back_section, cosine, sine_part).astype(jnp.bfloat16)
    result = product('dnck,clkb->dlnb', fourier_table(high_len, 1.0), turned)
    result = result * live_rows[None, :, None, None]
    return result.astype(jnp.bfloat16).reshape(2, line_total, RANGE)

def focus_columns(columns, filter_grid):
    line_total = columns.shape[1]
    col_width = columns.shape[2]
    inner_len = AZ_INNER
    outer_len = line_total // inner_len
    grid_data = columns.reshape(2, outer_len, inner_len, col_width)
    section_one = product('dkcm,cmbx->dkbx', fourier_table(outer_len, -1.0), grid_data)
    cosine, sine_part = twiddle(outer_len, inner_len, line_total, -1.0)
    rotated = rotate(section_one, cosine[:, :, None], sine_part[:, :, None]).astype(jnp.bfloat16)
    spectrum = product('dkcm,camx->dakx', fourier_table(inner_len, -1.0), rotated)
    shaped = jnp.stack([spectrum[0] * filter_grid[0] - spectrum[1] * filter_grid[1], spectrum[0] * filter_grid[1] + spectrum[1] * filter_grid[0]], axis=0).astype(jnp.bfloat16)
    back_section = product('dmck,cakx->damx', fourier_table(inner_len, 1.0), shaped)
    cosine, sine_part = twiddle(outer_len, inner_len, line_total, 1.0)
    turned = rotate(back_section, cosine[:, :, None], sine_part[:, :, None]).astype(jnp.bfloat16)
    result = product('dmck,ckbx->dmbx', fourier_table(outer_len, 1.0), turned)
    return result.astype(jnp.bfloat16).reshape(2, line_total, col_width)

def reference(raw_echo, valid_lines, range_filter, azimuth_filters, set_index):
    block_ids = jnp.arange(BLOCKS, dtype=jnp.int32)
    row_ids = jnp.arange(LINES_DEV, dtype=jnp.int32)

    def range_block(block_id):
        block = lax.dynamic_slice_in_dim(raw_echo, (block_id * LINES_DEV).astype(jnp.int32), LINES_DEV, 1)
        live_rows = (row_ids < valid_lines[block_id]).astype(jnp.float32)
        return compress_lines(block, live_rows, range_filter)
    pieces = lax.map(range_block, block_ids)
    compressed = pieces.transpose(1, 0, 2, 3).reshape(2, LINES, RANGE)
    filter_table = azimuth_filters.reshape(2, SETS, AZ_INNER, AZ_OUTER).transpose(0, 1, 3, 2)
    set_ids = jnp.arange(SETS, dtype=jnp.int32)

    def azimuth_block(block_id):
        start = (block_id * COLS).astype(jnp.int32)
        columns = lax.dynamic_slice_in_dim(compressed, start, COLS, 2)
        column_sets = lax.dynamic_slice_in_dim(set_index, start, COLS, 0)
        selector = (column_sets[:, None] == set_ids[None, :]).astype(jnp.float32)
        chosen = jnp.einsum('dsab,xs->dabx', filter_table, selector, precision=lax.Precision.HIGHEST)
        return focus_columns(columns, chosen)
    focused_parts = lax.map(azimuth_block, block_ids)
    return focused_parts.transpose(1, 2, 0, 3).reshape(2, LINES, RANGE)
```

```python
import functools
import math

import jax
import jax.numpy as jnp
from jax import lax
from jax.experimental import pallas as pl
from jax.experimental.pallas import tpu as pltpu
from jax.sharding import PartitionSpec as P

RANGE_LO = 256
AZ_INNER = 64
GROUP = 16
LANES = 128
CHUNK = 256
SLOTS = 4
STRIDE = 5


def fourier(length, sign_value):
    indices = jnp.arange(length, dtype=jnp.int32)
    phases = indices[:, None] * indices[None, :] % length
    angles = phases.astype(jnp.float32) * (2.0 * math.pi / length)
    return jnp.cos(angles), sign_value * jnp.sin(angles)


def left_table(length, sign_value):
    c, s = fourier(length, sign_value)
    return jnp.concatenate(
        [jnp.concatenate([c, -s], 1), jnp.concatenate([s, c], 1)], 0
    ).astype(jnp.bfloat16)


def right_table(length, sign_value):
    c, s = fourier(length, sign_value)
    return jnp.concatenate(
        [jnp.concatenate([c, s], 1), jnp.concatenate([-s, c], 1)], 0
    ).astype(jnp.bfloat16)


def twiddle(row_len, col_len, total_len):
    phases = (
        jnp.arange(row_len, dtype=jnp.int32)[:, None]
        * jnp.arange(col_len, dtype=jnp.int32)[None, :]
        % total_len
    )
    angles = phases.astype(jnp.float32) * (2.0 * math.pi / total_len)
    factor = 1.0 / math.sqrt(total_len)
    return jnp.stack([jnp.cos(angles) * factor, jnp.sin(angles) * factor])


def mul(m, x):
    return jnp.dot(m, x, preferred_element_type=jnp.float32)


def range_lines(first, live_ref, etab, vtab, ftab, xs, hi, lo):
    halves = lo // LANES

    def line(j, carry):
        def take(c):
            parts = [
                xs[c, h, pl.ds(j, hi, stride=GROUP), :].astype(jnp.bfloat16)
                for h in range(halves)
            ]
            return jnp.concatenate(parts, 1)

        x = jnp.concatenate([take(0), take(1)], 0)
        s = mul(etab[0], x)
        sr, si = s[:hi], s[hi:]
        vr, vi = vtab[0], vtab[1]
        q = jnp.concatenate(
            [
                (vr * sr + vi * si).astype(jnp.bfloat16),
                (vr * si - vi * sr).astype(jnp.bfloat16),
            ],
            1,
        )
        s = mul(q, etab[1])
        sr, si = s[:, :lo], s[:, lo:]
        fr, fi = ftab[0], ftab[1]
        q = jnp.concatenate(
            [
                (sr * fr - si * fi).astype(jnp.bfloat16),
                (sr * fi + si * fr).astype(jnp.bfloat16),
            ],
            1,
        )
        s = mul(q, etab[2])
        sr, si = s[:, :lo], s[:, lo:]
        z = jnp.concatenate(
            [
                (vr * sr - vi * si).astype(jnp.bfloat16),
                (vi * sr + vr * si).astype(jnp.bfloat16),
            ],
            0,
        )
        s = mul(etab[3], z) * live_ref[first + j]
        for h in range(halves):
            cols = slice(h * LANES, (h + 1) * LANES)
            xs[0, h, pl.ds(j, hi, stride=GROUP), :] = s[:hi, cols]
            xs[1, h, pl.ds(j, hi, stride=GROUP), :] = s[hi:, cols]
        return carry

    lax.fori_loop(0, GROUP, line, 0, unroll=2)


def place(devices):
    line_count = lax.axis_size("line")
    me = lax.axis_index("grp") * line_count + lax.axis_index("line")

    def peer(step):
        d = lax.rem(me + step * STRIDE, devices)
        return d, (lax.div(d, line_count), lax.rem(d, line_count))

    return me, peer


def greet(devices, peer):
    barrier = pltpu.get_barrier_semaphore()

    def signal(step, carry):
        pl.semaphore_signal(
            barrier, inc=1, device_id=peer(step)[1], device_id_type=pl.DeviceIdType.MESH
        )
        return carry

    lax.fori_loop(1, devices, signal, 0)
    pl.semaphore_wait(barrier, devices - 1)


def range_kernel(
    devices, live_ref, raw, etab, vtab, ftab, recv, xbuf, xs, stage, x_sem, own_sem, send_sem, recv_sem
):
    _, lines, cols = raw.shape
    width = recv.shape[-1]
    lo = vtab.shape[-1]
    hi = cols // lo
    halves = lo // LANES
    groups = lines // GROUP
    me, peer = place(devices)

    def fetch(g):
        rows = pl.ds(pl.multiple_of(g * GROUP, GROUP), GROUP)
        slot = lax.rem(g, 2)
        return pltpu.make_async_copy(raw.at[:, rows, :], xbuf.at[slot], x_sem.at[slot])

    def own_copy(g):
        rows = pl.ds(pl.multiple_of(g * GROUP, GROUP), GROUP)
        slot = lax.rem(g, SLOTS)
        mine = pl.ds(pl.multiple_of(me * width, width), width)
        return pltpu.make_async_copy(
            stage.at[slot, :, :, mine], recv.at[me, :, rows, :], own_sem.at[slot]
        )

    def drain(g):
        slot = lax.rem(g, SLOTS)
        own_copy(g).wait()
        sent = stage.at[slot, :, :, pl.ds(0, (devices - 1) * width)]
        pltpu.make_async_copy(sent, sent, send_sem.at[slot]).wait()

    fetch(0).start()
    greet(devices, peer)

    def group(g, carry):
        slot, now = lax.rem(g, SLOTS), lax.rem(g, 2)

        @pl.when(g + 1 < groups)
        def _():
            fetch(g + 1).start()

        fetch(g).wait()

        def load(n, carry):
            for c in range(2):
                for h in range(halves):
                    col = pl.multiple_of(n * lo + h * LANES, LANES)
                    row = pl.multiple_of(n * GROUP, GROUP)
                    xs[c, h, pl.ds(row, GROUP), :] = xbuf[now, c, :, pl.ds(col, LANES)].astype(
                        jnp.float32
                    )
            return carry

        lax.fori_loop(0, hi, load, 0, unroll=4)
        range_lines(g * GROUP, live_ref, etab, vtab, ftab, xs, hi, lo)

        @pl.when(g >= SLOTS)
        def _():
            drain(g - SLOTS)

        def save(n, carry):
            for c in range(2):
                for h in range(halves):
                    col = pl.multiple_of(n * lo + h * LANES, LANES)
                    row = pl.multiple_of(n * GROUP, GROUP)
                    stage[slot, c, :, pl.ds(col, LANES)] = xs[c, h, pl.ds(row, GROUP), :].astype(
                        jnp.bfloat16
                    )
            return carry

        lax.fori_loop(0, hi, save, 0, unroll=4)
        own_copy(g).start()

        def send(step, carry):
            d, target = peer(step)
            rows = pl.ds(pl.multiple_of(g * GROUP, GROUP), GROUP)
            pltpu.make_async_remote_copy(
                src_ref=stage.at[slot, :, :, pl.ds(pl.multiple_of(d * width, width), width)],
                dst_ref=recv.at[me, :, rows, :],
                send_sem=send_sem.at[slot],
                recv_sem=recv_sem.at[0],
                device_id=target,
                device_id_type=pl.DeviceIdType.MESH,
            ).start()
            return carry

        lax.fori_loop(1, devices, send, 0)
        return carry

    lax.fori_loop(0, groups, group, 0)
    for g in range(max(0, groups - SLOTS), groups):
        drain(jnp.int32(g))
    arrived = recv.at[pl.ds(0, devices - 1)]
    pltpu.make_async_copy(arrived, arrived, recv_sem.at[0]).wait()


def compress(raw, live, etab, vtab, ftab, devices):
    _, lines, cols = raw.shape
    lo = RANGE_LO
    hi = cols // lo
    vmem = pl.BlockSpec(memory_space=pltpu.VMEM)
    hbm = pl.BlockSpec(memory_space=pl.ANY)
    return pl.pallas_call(
        functools.partial(range_kernel, devices),
        out_shape=jax.ShapeDtypeStruct((devices, 2, lines, cols // devices), jnp.bfloat16),
        in_specs=[pl.BlockSpec(memory_space=pltpu.SMEM), hbm, vmem, vmem, vmem],
        out_specs=hbm,
        scratch_shapes=[
            pltpu.VMEM((2, 2, GROUP, cols), jnp.bfloat16),
            pltpu.VMEM((2, lo // LANES, hi * GROUP, LANES), jnp.float32),
            pltpu.VMEM((SLOTS, 2, GROUP, cols), jnp.bfloat16),
            pltpu.SemaphoreType.DMA((2,)),
            pltpu.SemaphoreType.DMA((SLOTS,)),
            pltpu.SemaphoreType.DMA((SLOTS,)),
            pltpu.SemaphoreType.DMA((1,)),
        ],
        compiler_params=pltpu.CompilerParams(
            vmem_limit_bytes=56 << 20, collective_id=0, has_side_effects=True
        ),
        name="range_compress",
    )(live, raw, etab, vtab, ftab)


def azimuth_columns(etab, ttab, filt, pick, us, outer, inner):
    halves = CHUNK // LANES

    def take(rows):
        return jnp.concatenate(
            [
                jnp.concatenate(
                    [us[c, h, rows, :].astype(jnp.bfloat16) for h in range(halves)], 1
                )
                for c in range(2)
            ],
            0,
        )

    def put(rows, h, re, im):
        us[0, h, rows, :] = re
        us[1, h, rows, :] = im

    def first(m, carry):
        rows = pl.ds(m, outer, stride=inner)
        s = mul(etab[0], take(rows))
        vr, vi = ttab[0, m], ttab[1, m]
        for h in range(halves):
            cols = slice(h * LANES, (h + 1) * LANES)
            sr, si = s[:outer, cols], s[outer:, cols]
            put(rows, h, vr * sr + vi * si, vr * si - vi * sr)
        return carry

    def second(k, carry):
        rows = pl.ds(pl.multiple_of(k * inner, inner), inner)
        s = mul(etab[0], take(rows))
        f = mul(filt[k], pick)
        sr, si = s[:inner], s[inner:]
        fr, fi = f[:inner], f[inner:]
        b = jnp.concatenate(
            [
                (sr * fr - si * fi).astype(jnp.bfloat16),
                (sr * fi + si * fr).astype(jnp.bfloat16),
            ],
            0,
        )
        s = mul(etab[1], b)
        vr, vi = ttab[0, k], ttab[1, k]
        for h in range(halves):
            cols = slice(h * LANES, (h + 1) * LANES)
            sr, si = s[:inner, cols], s[inner:, cols]
            put(rows, h, vr * sr - vi * si, vi * sr + vr * si)
        return carry

    def last(m, carry):
        rows = pl.ds(m, outer, stride=inner)
        s = mul(etab[1], take(rows))
        for h in range(halves):
            cols = slice(h * LANES, (h + 1) * LANES)
            put(rows, h, s[:outer, cols], s[outer:, cols])
        return carry

    lax.fori_loop(0, inner, first, 0, unroll=4)
    lax.fori_loop(0, outer, second, 0, unroll=4)
    lax.fori_loop(0, inner, last, 0, unroll=4)


def pick_rows(sets_row, sets):
    row = lax.broadcasted_iota(jnp.int32, (3 * sets, CHUNK), 0) % sets
    return jnp.where(row == sets_row, 1.0, 0.0).astype(jnp.bfloat16)


def azimuth_kernel(
    devices, sets, s_ref, columns, etab, ttab, filt, out, ubuf, us, stage, u_sem, own_sem, send_sem, recv_sem
):
    _, _, lines, width = columns.shape
    inner = AZ_INNER
    outer = devices * lines // inner
    halves = CHUNK // LANES
    chunks = width // CHUNK
    me, peer = place(devices)

    def fetch(j):
        cols = pl.ds(pl.multiple_of(j * CHUNK, CHUNK), CHUNK)
        slot = lax.rem(j, 2)
        return pltpu.make_async_copy(columns.at[:, :, :, cols], ubuf.at[slot], u_sem.at[slot])

    def home(j):
        return out.at[:, :, pl.ds(pl.multiple_of(me * width + j * CHUNK, CHUNK), CHUNK)]

    def own_copy(j):
        slot = lax.rem(j, SLOTS)
        return pltpu.make_async_copy(stage.at[slot, me], home(j), own_sem.at[slot])

    def drain(j):
        slot = lax.rem(j, SLOTS)
        own_copy(j).wait()
        sent = stage.at[slot, pl.ds(0, devices - 1)]
        pltpu.make_async_copy(sent, sent, send_sem.at[slot]).wait()

    fetch(0).start()
    greet(devices, peer)

    def chunk(j, carry):
        slot, now = lax.rem(j, SLOTS), lax.rem(j, 2)

        @pl.when(j + 1 < chunks)
        def _():
            fetch(j + 1).start()

        fetch(j).wait()

        def load(b, carry):
            for c in range(2):
                for h in range(halves):
                    row = pl.multiple_of(b * lines, lines)
                    us[c, h, pl.ds(row, lines), :] = ubuf[
                        now, b, c, :, h * LANES : (h + 1) * LANES
                    ].astype(jnp.float32)
            return carry

        lax.fori_loop(0, devices, load, 0)
        pick = pick_rows(s_ref[j], sets)
        azimuth_columns(etab, ttab, filt, pick, us, outer, inner)

        @pl.when(j >= SLOTS)
        def _():
            drain(j - SLOTS)

        def save(b, carry):
            for c in range(2):
                for h in range(halves):
                    row = pl.multiple_of(b * lines, lines)
                    stage[slot, b, c, :, h * LANES : (h + 1) * LANES] = us[
                        c, h, pl.ds(row, lines), :
                    ].astype(jnp.bfloat16)
            return carry

        lax.fori_loop(0, devices, save, 0)
        own_copy(j).start()

        def send(step, carry):
            d, target = peer(step)
            pltpu.make_async_remote_copy(
                src_ref=stage.at[slot, d],
                dst_ref=home(j),
                send_sem=send_sem.at[slot],
                recv_sem=recv_sem.at[0],
                device_id=target,
                device_id_type=pl.DeviceIdType.MESH,
            ).start()
            return carry

        lax.fori_loop(1, devices, send, 0)
        return carry

    lax.fori_loop(0, chunks, chunk, 0)
    for j in range(max(0, chunks - SLOTS), chunks):
        drain(jnp.int32(j))
    arrived = out.at[:, :, pl.ds(0, (devices - 1) * width)]
    pltpu.make_async_copy(arrived, arrived, recv_sem.at[0]).wait()


def focus(columns, column_sets, etab, ttab, filt, sets):
    devices, _, lines, width = columns.shape
    vmem = pl.BlockSpec(memory_space=pltpu.VMEM)
    hbm = pl.BlockSpec(memory_space=pl.ANY)
    return pl.pallas_call(
        functools.partial(azimuth_kernel, devices, sets),
        out_shape=jax.ShapeDtypeStruct((2, lines, devices * width), jnp.bfloat16),
        in_specs=[vmem, hbm, vmem, vmem, vmem],
        out_specs=hbm,
        scratch_shapes=[
            pltpu.VMEM((2, devices, 2, lines, CHUNK), jnp.bfloat16),
            pltpu.VMEM((2, CHUNK // LANES, devices * lines, LANES), jnp.float32),
            pltpu.VMEM((SLOTS, devices, 2, lines, CHUNK), jnp.bfloat16),
            pltpu.SemaphoreType.DMA((2,)),
            pltpu.SemaphoreType.DMA((SLOTS,)),
            pltpu.SemaphoreType.DMA((SLOTS,)),
            pltpu.SemaphoreType.DMA((1,)),
        ],
        compiler_params=pltpu.CompilerParams(
            vmem_limit_bytes=56 << 20, collective_id=1, has_side_effects=True
        ),
        name="azimuth_focus",
    )(column_sets, columns, etab, ttab, filt)


def per_device(raw_echo, valid_lines, range_filter, azimuth_filters, set_index):
    _, lines, cols = raw_echo.shape
    line_count = lax.axis_size("line")
    devices = lax.axis_size("grp") * line_count
    block_id = lax.axis_index("grp") * line_count + lax.axis_index("line")
    lo = RANGE_LO
    hi = cols // lo
    width = cols // devices
    inner = AZ_INNER
    outer = devices * lines // inner
    assert hi == lo and outer == inner

    live = (jnp.arange(lines, dtype=jnp.int32) < valid_lines[block_id]).astype(jnp.float32)
    etab = jnp.stack(
        [left_table(hi, -1.0), right_table(lo, -1.0), right_table(lo, 1.0), left_table(hi, 1.0)]
    )
    vtab = twiddle(hi, lo, cols)
    ftab = range_filter.reshape(2, lo, hi).transpose(0, 2, 1)
    columns = compress(raw_echo, live, etab, vtab, ftab, devices)

    sets = azimuth_filters.shape[1]
    aztab = jnp.stack([left_table(inner, -1.0), left_table(inner, 1.0)])
    ttab = jnp.broadcast_to(
        twiddle(inner, outer, inner * outer)[..., None], (2, inner, outer, LANES)
    )
    filt = azimuth_filters.reshape(2, sets, inner, outer).transpose(3, 0, 2, 1)
    filt = filt.reshape(outer, 2 * inner, sets)
    high = lax.reduce_precision(filt, 8, 7)
    mid = lax.reduce_precision(filt - high, 8, 7)
    low = filt - high - mid
    filt = jnp.concatenate([high, mid, low], -1).astype(jnp.bfloat16)
    column_sets = lax.dynamic_slice_in_dim(set_index, block_id * width, width, 0)
    column_sets = column_sets.reshape(width // CHUNK, 1, CHUNK)
    return focus(columns, column_sets, aztab, ttab, filt, sets)


def solution(mesh):
    placed = (P(None, ("grp", "line"), None), P(), P(), P(), P())
    return jax.shard_map(
        per_device,
        mesh=mesh,
        in_specs=placed,
        out_specs=P(None, ("grp", "line"), None),
        check_vma=False,
    )
```

```python
import functools
import math

import jax
import jax.numpy as jnp
import numpy as np
from jax import lax
from jax.experimental import pallas as pl
from jax.experimental.pallas import tpu as pltpu
from jax.sharding import PartitionSpec as P

RANGE_LO = 256
AZ_INNER = 64
GROUP = 16
LANES = 128
CHUNK = 256
SLOTS = 4
STRIDE = 5


def fourier(length, sign_value):
    indices = np.arange(length, dtype=np.int64)
    phases = indices[:, None] * indices[None, :] % length
    angles = phases.astype(np.float32) * (2.0 * math.pi / length)
    return np.cos(angles), sign_value * np.sin(angles)


def left_table(length, sign_value):
    c, s = fourier(length, sign_value)
    return np.concatenate(
        [np.concatenate([c, -s], 1), np.concatenate([s, c], 1)], 0
    )


def right_table(length, sign_value):
    c, s = fourier(length, sign_value)
    return np.concatenate(
        [np.concatenate([c, s], 1), np.concatenate([-s, c], 1)], 0
    )


def twiddle(row_len, col_len, total_len):
    phases = (
        np.arange(row_len, dtype=np.int64)[:, None]
        * np.arange(col_len, dtype=np.int64)[None, :]
        % total_len
    )
    angles = phases.astype(np.float32) * (2.0 * math.pi / total_len)
    factor = 1.0 / math.sqrt(total_len)
    return np.stack([np.cos(angles) * factor, np.sin(angles) * factor]).astype(np.float32)


def mul(m, x):
    return jnp.dot(m, x, preferred_element_type=jnp.float32)


def range_lines(first, live_ref, etab, vtab, ftab, xs, hi, lo):
    halves = lo // LANES

    def line(j, carry):
        def take(c):
            parts = [
                xs[c, h, pl.ds(j, hi, stride=GROUP), :].astype(jnp.bfloat16)
                for h in range(halves)
            ]
            return jnp.concatenate(parts, 1)

        x = jnp.concatenate([take(0), take(1)], 0)
        s = mul(etab[0], x)
        sr, si = s[:hi], s[hi:]
        vr, vi = vtab[0], vtab[1]
        q = jnp.concatenate(
            [
                (vr * sr + vi * si).astype(jnp.bfloat16),
                (vr * si - vi * sr).astype(jnp.bfloat16),
            ],
            1,
        )
        s = mul(q, etab[1])
        sr, si = s[:, :lo], s[:, lo:]
        fr, fi = ftab[0], ftab[1]
        q = jnp.concatenate(
            [
                (sr * fr - si * fi).astype(jnp.bfloat16),
                (sr * fi + si * fr).astype(jnp.bfloat16),
            ],
            1,
        )
        s = mul(q, etab[2])
        sr, si = s[:, :lo], s[:, lo:]
        z = jnp.concatenate(
            [
                (vr * sr - vi * si).astype(jnp.bfloat16),
                (vi * sr + vr * si).astype(jnp.bfloat16),
            ],
            0,
        )
        s = mul(etab[3], z) * live_ref[first + j]
        for h in range(halves):
            cols = slice(h * LANES, (h + 1) * LANES)
            xs[0, h, pl.ds(j, hi, stride=GROUP), :] = s[:hi, cols]
            xs[1, h, pl.ds(j, hi, stride=GROUP), :] = s[hi:, cols]
        return carry

    lax.fori_loop(0, GROUP, line, 0, unroll=2)


def place(devices):
    line_count = lax.axis_size("line")
    me = lax.axis_index("grp") * line_count + lax.axis_index("line")

    def peer(step):
        d = lax.rem(me + step * STRIDE, devices)
        return d, (lax.div(d, line_count), lax.rem(d, line_count))

    return me, peer


def greet(devices, peer):
    barrier = pltpu.get_barrier_semaphore()

    def signal(step, carry):
        pl.semaphore_signal(
            barrier, inc=1, device_id=peer(step)[1], device_id_type=pl.DeviceIdType.MESH
        )
        return carry

    lax.fori_loop(1, devices, signal, 0)
    pl.semaphore_wait(barrier, devices - 1)


def range_kernel(
    devices, live_ref, raw, etab, vtab, ftab, recv, xbuf, xs, stage, x_sem, own_sem, send_sem, recv_sem
):
    _, lines, cols = raw.shape
    width = recv.shape[-1]
    lo = vtab.shape[-1]
    hi = cols // lo
    halves = lo // LANES
    groups = lines // GROUP
    me, peer = place(devices)

    def fetch(g):
        rows = pl.ds(pl.multiple_of(g * GROUP, GROUP), GROUP)
        slot = lax.rem(g, 2)
        return pltpu.make_async_copy(raw.at[:, rows, :], xbuf.at[slot], x_sem.at[slot])

    def own_copy(g):
        rows = pl.ds(pl.multiple_of(g * GROUP, GROUP), GROUP)
        slot = lax.rem(g, SLOTS)
        mine = pl.ds(pl.multiple_of(me * width, width), width)
        return pltpu.make_async_copy(
            stage.at[slot, :, :, mine], recv.at[me, :, rows, :], own_sem.at[slot]
        )

    def drain(g):
        slot = lax.rem(g, SLOTS)
        own_copy(g).wait()
        sent = stage.at[slot, :, :, pl.ds(0, (devices - 1) * width)]
        pltpu.make_async_copy(sent, sent, send_sem.at[slot]).wait()

    fetch(0).start()
    greet(devices, peer)

    def group(g, carry):
        slot, now = lax.rem(g, SLOTS), lax.rem(g, 2)

        @pl.when(g + 1 < groups)
        def _():
            fetch(g + 1).start()

        fetch(g).wait()

        def load(n, carry):
            for c in range(2):
                for h in range(halves):
                    col = pl.multiple_of(n * lo + h * LANES, LANES)
                    row = pl.multiple_of(n * GROUP, GROUP)
                    xs[c, h, pl.ds(row, GROUP), :] = xbuf[now, c, :, pl.ds(col, LANES)].astype(
                        jnp.float32
                    )
            return carry

        lax.fori_loop(0, hi, load, 0, unroll=4)
        range_lines(g * GROUP, live_ref, etab, vtab, ftab, xs, hi, lo)

        @pl.when(g >= SLOTS)
        def _():
            drain(g - SLOTS)

        def save(n, carry):
            for c in range(2):
                for h in range(halves):
                    col = pl.multiple_of(n * lo + h * LANES, LANES)
                    row = pl.multiple_of(n * GROUP, GROUP)
                    stage[slot, c, :, pl.ds(col, LANES)] = xs[c, h, pl.ds(row, GROUP), :].astype(
                        jnp.bfloat16
                    )
            return carry

        lax.fori_loop(0, hi, save, 0, unroll=4)
        own_copy(g).start()

        def send(step, carry):
            d, target = peer(step)
            rows = pl.ds(pl.multiple_of(g * GROUP, GROUP), GROUP)
            pltpu.make_async_remote_copy(
                src_ref=stage.at[slot, :, :, pl.ds(pl.multiple_of(d * width, width), width)],
                dst_ref=recv.at[me, :, rows, :],
                send_sem=send_sem.at[slot],
                recv_sem=recv_sem.at[0],
                device_id=target,
                device_id_type=pl.DeviceIdType.MESH,
            ).start()
            return carry

        lax.fori_loop(1, devices, send, 0)
        return carry

    lax.fori_loop(0, groups, group, 0)
    for g in range(max(0, groups - SLOTS), groups):
        drain(jnp.int32(g))
    arrived = recv.at[pl.ds(0, devices - 1)]
    pltpu.make_async_copy(arrived, arrived, recv_sem.at[0]).wait()


def compress(raw, live, etab, vtab, ftab, devices):
    _, lines, cols = raw.shape
    lo = RANGE_LO
    hi = cols // lo
    vmem = pl.BlockSpec(memory_space=pltpu.VMEM)
    hbm = pl.BlockSpec(memory_space=pl.ANY)
    return pl.pallas_call(
        functools.partial(range_kernel, devices),
        out_shape=jax.ShapeDtypeStruct((devices, 2, lines, cols // devices), jnp.bfloat16),
        in_specs=[pl.BlockSpec(memory_space=pltpu.SMEM), hbm, vmem, vmem, vmem],
        out_specs=hbm,
        scratch_shapes=[
            pltpu.VMEM((2, 2, GROUP, cols), jnp.bfloat16),
            pltpu.VMEM((2, lo // LANES, hi * GROUP, LANES), jnp.float32),
            pltpu.VMEM((SLOTS, 2, GROUP, cols), jnp.bfloat16),
            pltpu.SemaphoreType.DMA((2,)),
            pltpu.SemaphoreType.DMA((SLOTS,)),
            pltpu.SemaphoreType.DMA((SLOTS,)),
            pltpu.SemaphoreType.DMA((1,)),
        ],
        compiler_params=pltpu.CompilerParams(
            vmem_limit_bytes=56 << 20, collective_id=0, has_side_effects=True
        ),
        name="range_compress",
    )(live, raw, etab, vtab, ftab)


def azimuth_columns(etab, ttab, filt, pick, us, outer, inner):
    halves = CHUNK // LANES

    def take(rows):
        return jnp.concatenate(
            [
                jnp.concatenate(
                    [us[c, h, rows, :].astype(jnp.bfloat16) for h in range(halves)], 1
                )
                for c in range(2)
            ],
            0,
        )

    def put(rows, h, re, im):
        us[0, h, rows, :] = re
        us[1, h, rows, :] = im

    def first(m, carry):
        rows = pl.ds(m, outer, stride=inner)
        s = mul(etab[0], take(rows))
        vr, vi = ttab[0, m], ttab[1, m]
        for h in range(halves):
            cols = slice(h * LANES, (h + 1) * LANES)
            sr, si = s[:outer, cols], s[outer:, cols]
            put(rows, h, vr * sr + vi * si, vr * si - vi * sr)
        return carry

    def second(k, carry):
        rows = pl.ds(pl.multiple_of(k * inner, inner), inner)
        s = mul(etab[0], take(rows))
        f = mul(filt[k], pick)
        sr, si = s[:inner], s[inner:]
        fr, fi = f[:inner], f[inner:]
        b = jnp.concatenate(
            [
                (sr * fr - si * fi).astype(jnp.bfloat16),
                (sr * fi + si * fr).astype(jnp.bfloat16),
            ],
            0,
        )
        s = mul(etab[1], b)
        vr, vi = ttab[0, k], ttab[1, k]
        for h in range(halves):
            cols = slice(h * LANES, (h + 1) * LANES)
            sr, si = s[:inner, cols], s[inner:, cols]
            put(rows, h, vr * sr - vi * si, vi * sr + vr * si)
        return carry

    def last(m, carry):
        rows = pl.ds(m, outer, stride=inner)
        s = mul(etab[1], take(rows))
        for h in range(halves):
            cols = slice(h * LANES, (h + 1) * LANES)
            put(rows, h, s[:outer, cols], s[outer:, cols])
        return carry

    lax.fori_loop(0, inner, first, 0, unroll=4)
    lax.fori_loop(0, outer, second, 0, unroll=4)
    lax.fori_loop(0, inner, last, 0, unroll=4)


def pick_rows(sets_row, sets):
    row = lax.broadcasted_iota(jnp.int32, (3 * sets, CHUNK), 0) % sets
    return jnp.where(row == sets_row, 1.0, 0.0).astype(jnp.bfloat16)


def azimuth_kernel(
    devices, sets, s_ref, columns, etab, ttab, filt, out, ubuf, us, stage, u_sem, own_sem, send_sem, recv_sem
):
    _, _, lines, width = columns.shape
    inner = AZ_INNER
    outer = devices * lines // inner
    halves = CHUNK // LANES
    chunks = width // CHUNK
    me, peer = place(devices)

    def fetch(j):
        cols = pl.ds(pl.multiple_of(j * CHUNK, CHUNK), CHUNK)
        slot = lax.rem(j, 2)
        return pltpu.make_async_copy(columns.at[:, :, :, cols], ubuf.at[slot], u_sem.at[slot])

    def home(j):
        return out.at[:, :, pl.ds(pl.multiple_of(me * width + j * CHUNK, CHUNK), CHUNK)]

    def own_copy(j):
        slot = lax.rem(j, SLOTS)
        return pltpu.make_async_copy(stage.at[slot, me], home(j), own_sem.at[slot])

    def drain(j):
        slot = lax.rem(j, SLOTS)
        own_copy(j).wait()
        sent = stage.at[slot, pl.ds(0, devices - 1)]
        pltpu.make_async_copy(sent, sent, send_sem.at[slot]).wait()

    fetch(0).start()
    greet(devices, peer)

    def chunk(j, carry):
        slot, now = lax.rem(j, SLOTS), lax.rem(j, 2)

        @pl.when(j + 1 < chunks)
        def _():
            fetch(j + 1).start()

        fetch(j).wait()

        def load(b, carry):
            for c in range(2):
                for h in range(halves):
                    row = pl.multiple_of(b * lines, lines)
                    us[c, h, pl.ds(row, lines), :] = ubuf[
                        now, b, c, :, h * LANES : (h + 1) * LANES
                    ].astype(jnp.float32)
            return carry

        lax.fori_loop(0, devices, load, 0)
        pick = pick_rows(s_ref[j], sets)
        azimuth_columns(etab, ttab, filt, pick, us, outer, inner)

        @pl.when(j >= SLOTS)
        def _():
            drain(j - SLOTS)

        def save(b, carry):
            for c in range(2):
                for h in range(halves):
                    row = pl.multiple_of(b * lines, lines)
                    stage[slot, b, c, :, h * LANES : (h + 1) * LANES] = us[
                        c, h, pl.ds(row, lines), :
                    ].astype(jnp.bfloat16)
            return carry

        lax.fori_loop(0, devices, save, 0)
        own_copy(j).start()

        def send(step, carry):
            d, target = peer(step)
            pltpu.make_async_remote_copy(
                src_ref=stage.at[slot, d],
                dst_ref=home(j),
                send_sem=send_sem.at[slot],
                recv_sem=recv_sem.at[0],
                device_id=target,
                device_id_type=pl.DeviceIdType.MESH,
            ).start()
            return carry

        lax.fori_loop(1, devices, send, 0)
        return carry

    lax.fori_loop(0, chunks, chunk, 0)
    for j in range(max(0, chunks - SLOTS), chunks):
        drain(jnp.int32(j))
    arrived = out.at[:, :, pl.ds(0, (devices - 1) * width)]
    pltpu.make_async_copy(arrived, arrived, recv_sem.at[0]).wait()


def focus(columns, column_sets, etab, ttab, filt, sets):
    devices, _, lines, width = columns.shape
    vmem = pl.BlockSpec(memory_space=pltpu.VMEM)
    hbm = pl.BlockSpec(memory_space=pl.ANY)
    return pl.pallas_call(
        functools.partial(azimuth_kernel, devices, sets),
        out_shape=jax.ShapeDtypeStruct((2, lines, devices * width), jnp.bfloat16),
        in_specs=[vmem, hbm, vmem, vmem, vmem],
        out_specs=hbm,
        scratch_shapes=[
            pltpu.VMEM((2, devices, 2, lines, CHUNK), jnp.bfloat16),
            pltpu.VMEM((2, CHUNK // LANES, devices * lines, LANES), jnp.float32),
            pltpu.VMEM((SLOTS, devices, 2, lines, CHUNK), jnp.bfloat16),
            pltpu.SemaphoreType.DMA((2,)),
            pltpu.SemaphoreType.DMA((SLOTS,)),
            pltpu.SemaphoreType.DMA((SLOTS,)),
            pltpu.SemaphoreType.DMA((1,)),
        ],
        compiler_params=pltpu.CompilerParams(
            vmem_limit_bytes=56 << 20, collective_id=1, has_side_effects=True
        ),
        name="azimuth_focus",
    )(column_sets, columns, etab, ttab, filt)


def per_device(raw_echo, valid_lines, range_filter, azimuth_filters, set_index):
    _, lines, cols = raw_echo.shape
    line_count = lax.axis_size("line")
    devices = lax.axis_size("grp") * line_count
    block_id = lax.axis_index("grp") * line_count + lax.axis_index("line")
    lo = RANGE_LO
    hi = cols // lo
    width = cols // devices
    inner = AZ_INNER
    outer = devices * lines // inner
    assert hi == lo and outer == inner

    live = (jnp.arange(lines, dtype=jnp.int32) < valid_lines[block_id]).astype(jnp.float32)
    etab = np.stack(
        [left_table(hi, -1.0), right_table(lo, -1.0), right_table(lo, 1.0), left_table(hi, 1.0)]
    ).astype(jnp.bfloat16)
    etab, vtab = jnp.asarray(etab), jnp.asarray(twiddle(hi, lo, cols))
    ftab = range_filter.reshape(2, lo, hi).transpose(0, 2, 1)
    columns = compress(raw_echo, live, etab, vtab, ftab, devices)

    sets = azimuth_filters.shape[1]
    aztab = np.stack([left_table(inner, -1.0), left_table(inner, 1.0)])
    aztab = jnp.asarray(aztab.astype(jnp.bfloat16))
    ttab = jnp.broadcast_to(
        jnp.asarray(twiddle(inner, outer, inner * outer))[..., None], (2, inner, outer, LANES)
    )
    filt = azimuth_filters.reshape(2, sets, inner, outer).transpose(3, 0, 2, 1)
    filt = filt.reshape(outer, 2 * inner, sets)
    high = lax.reduce_precision(filt, 8, 7)
    mid = lax.reduce_precision(filt - high, 8, 7)
    low = filt - high - mid
    filt = jnp.concatenate([high, mid, low], -1).astype(jnp.bfloat16)
    column_sets = lax.dynamic_slice_in_dim(set_index, block_id * width, width, 0)
    column_sets = column_sets.reshape(width // CHUNK, 1, CHUNK)
    return focus(columns, column_sets, aztab, ttab, filt, sets)


def solution(mesh):
    placed = (P(None, ("grp", "line"), None), P(), P(), P(), P())
    return jax.shard_map(
        per_device,
        mesh=mesh,
        in_specs=placed,
        out_specs=P(None, ("grp", "line"), None),
        check_vma=False,
    )
```
